32 devices in a mesh: seq: 32 (over z, y, x, core).
Axes of the slice: x: 2, y: 2, z: 4, core: 2. Of those that a mesh axis runs over, the one named last changes fastest.
Arguments:
- queries: bfloat16 [32768, 1024], P('seq'), may hold values from -6 to 6
- keys_values: bfloat16 [32768, 2, 1024], P('seq'), may hold values from -6 to 6
- memory: bfloat16 [128, 64, 256], P('seq'), may hold values from -6 to 6
- block_regions: int32 [512, 4], P('seq'), may hold values from 0 to 127, as said below
- region_slot: int32 [128], replicated, may hold values from 0 to 127, as said below
- grad_out: bfloat16 [32768, 1024], P('seq'), may hold values from -6 to 6
Outputs:
- attended: bfloat16 [32768, 1024], P('seq')
- grad_queries: bfloat16 [32768, 1024], P('seq')
- grad_keys_values: bfloat16 [32768, 2, 1024], P('seq')
The draws below stay inside these ranges and needn't reach their ends.
Inputs may be any that keep to these rules, and one draw needn't show every extreme that they name: `block_regions`: each block names 4 different regions, and all regions named by the 16 blocks of one device are different. Of the regions named on one device, at most 2 are stored on any one device (the row region_slot[r] of memory lies on device region_slot[r] // 4); in every draw some device stores exactly 2 of the regions named on every device. `region_slot`: A permutation of the regions.
All inputs are finite; a program needn't handle non-finite values.
Results may differ from the reference program's by a relative error of at most 0.0062.
Values may be sent and summed in bfloat16 or wider, within the bound.
A program may use at most 192 MiB of HBM per device.

```python
import math
import jax
import jax.numpy as jnp
from jax import lax

H = 8
DH = 128
D = 1024
BLK = 64
WIN = 2
MEM = 4
BLK_DEV = 16
REG_DEV = 4
TOKENS = 32768
NBLK = 512
REGIONS = 128


def drawn_rows(key):
    values = jnp.clip(jax.random.normal(jax.random.fold_in(key, 5), (TOKENS, D), dtype=jnp.float32), -6.0, 6.0)
    return values


def draw_queries(key, part):
    values = drawn_rows(jax.random.fold_in(key, 21))
    return values.astype(jnp.bfloat16)


def draw_keys_values(key, part):
    key_part = drawn_rows(jax.random.fold_in(key, 31))
    value_part = drawn_rows(jax.random.fold_in(key, 32))
    return jnp.stack([key_part, value_part], axis=1).astype(jnp.bfloat16)


def draw_region_slot(key, part):
    return jax.random.permutation(jax.random.fold_in(key, 11), REGIONS).astype(jnp.int32)


def draw_block_regions(key, part):
    slot_of = draw_region_slot(key, part)
    region_of = jnp.argsort(slot_of).astype(jnp.int32)
    owners = REGIONS // REG_DEV
    ref_count = BLK_DEV * MEM
    hot_owner = jax.random.randint(jax.random.fold_in(key, 12), (), 0, owners)

    def device_refs(device_id):
        device_key = jax.random.fold_in(jax.random.fold_in(key, 13), device_id)
        others = jax.random.permutation(jax.random.fold_in(device_key, 1), owners - 1).astype(jnp.int32) + 1
        spread = jnp.concatenate([jnp.zeros((1,), jnp.int32), others])
        ref_order = jnp.arange(ref_count, dtype=jnp.int32)
        owner_dev = (hot_owner + spread[ref_order % owners]) % owners
        offsets = jax.random.randint(jax.random.fold_in(device_key, 2), (owners,), 0, REG_DEV)
        local_row = (offsets[ref_order % owners] + ref_order // owners) % REG_DEV
        return region_of[owner_dev * REG_DEV + local_row]
    table = jax.vmap(device_refs)(jnp.arange(owners, dtype=jnp.int32))
    return table.reshape(NBLK, MEM).astype(jnp.int32)


def block_levels(stream_key, extent, shards, low, high):
    level = 1.0
    for position, shards_of in shards:
        steps = jax.random.uniform(jax.random.fold_in(jax.random.fold_in(stream_key, 6), position), (shards_of,), jnp.float32, low / len(shards), high / len(shards))
        level = level * jnp.repeat(jnp.exp(steps), extent[position] // shards_of).reshape((-1,) + (1,) * (len(extent) - 1 - position))
    return level


def bell_draw(stream_key, dims, width, bound, split=(), kind=jnp.bfloat16):
    loudness = block_levels(stream_key, dims, split, -0.22, 0.18) if split else 1.0
    result = jax.random.normal(stream_key, dims, jnp.float32) * width * loudness
    return jnp.minimum(jnp.maximum(result, -bound), bound).astype(kind)


def setup_inputs(seed: int = 0) -> dict:
    splits = jax.random.split(jax.random.key(seed), 7)
    queries = draw_queries(jax.random.fold_in(splits[6], 71), 0)
    keys_values = draw_keys_values(jax.random.fold_in(splits[6], 71), 0)
    memory = bell_draw(splits[2], (REGIONS, BLK, 2 * DH), 1.0, 6.0, ((0, 32),))
    block_regions = draw_block_regions(jax.random.fold_in(splits[6], 71), 0)
    region_slot = draw_region_slot(jax.random.fold_in(splits[6], 71), 0)
    grad_out = bell_draw(splits[5], (TOKENS, D), 1.0, 6.0, ((0, 32),))
    return {"queries": queries, "keys_values": keys_values, "memory": memory, "block_regions": block_regions, "region_slot": region_slot, "grad_out": grad_out}


NEG_FILL = -1e+30

def reference(queries, keys_values, memory, block_regions, region_slot, grad_out):
    window_span = 2 * WIN + 1
    score_scale = 1.0 / math.sqrt(DH)
    highest = lax.Precision.HIGHEST
    kv_padded = jnp.pad(keys_values, ((WIN * BLK, WIN * BLK), (0, 0), (0, 0)))

    def query_block(block_id):
        row_first = block_id * BLK
        query_rows = lax.dynamic_slice_in_dim(queries, row_first, BLK, 0).astype(jnp.float32).reshape(BLK, H, DH)
        grad_rows = lax.dynamic_slice_in_dim(grad_out, row_first, BLK, 0).astype(jnp.float32).reshape(BLK, H, DH)
        window = lax.dynamic_slice_in_dim(kv_padded, row_first, window_span * BLK, 0)
        window = window.astype(jnp.float32).reshape(window_span * BLK, 2, H, DH)
        memory_rows = memory[region_slot[block_regions[block_id]]].astype(jnp.float32).reshape(MEM * BLK, 2 * DH)
        mem_keys = jnp.broadcast_to(memory_rows[:, None, :DH], (MEM * BLK, H, DH))
        mem_values = jnp.broadcast_to(memory_rows[:, None, DH:], (MEM * BLK, H, DH))
        all_keys = jnp.concatenate([window[:, 0], mem_keys], axis=0)
        all_values = jnp.concatenate([window[:, 1], mem_values], axis=0)
        neighbour = block_id + jnp.arange(window_span, dtype=jnp.int32) - WIN
        inside = (neighbour >= 0) & (neighbour < NBLK)
        valid_keys = jnp.concatenate([jnp.repeat(inside, BLK), jnp.ones((MEM * BLK,), dtype=jnp.bool_)])
        scores = jnp.einsum('ihe,jhe->hij', query_rows, all_keys, precision=highest) * score_scale
        scores = jnp.where(valid_keys[None, None, :], scores, NEG_FILL)
        row_max = lax.optimization_barrier(jnp.max(scores, axis=-1, keepdims=True))
        exp_scores = jnp.exp(scores - row_max)
        totals = lax.optimization_barrier(jnp.sum(exp_scores, axis=-1, keepdims=True))
        weights = exp_scores / totals
        weights_low = lax.optimization_barrier(weights.astype(jnp.bfloat16)).astype(jnp.float32)
        attended = jnp.einsum('hij,jhe->ihe', weights_low, all_values, precision=highest).astype(jnp.bfloat16)
        grad_probs = jnp.einsum('ihe,jhe->hij', grad_rows, all_values, precision=highest)
        row_delta = lax.optimization_barrier(jnp.sum(weights * grad_probs, axis=-1))
        grad_scores = weights * (grad_probs - row_delta[..., None])
        grad_low = lax.optimization_barrier(grad_scores.astype(jnp.bfloat16)).astype(jnp.float32)
        grad_query = jnp.einsum('hij,jhe->ihe', grad_low, all_keys, precision=highest) * score_scale
        log_total = row_max[..., 0] + jnp.log(totals[..., 0])
        return (attended, grad_query.astype(jnp.bfloat16), log_total, row_delta)
    attended, grad_query, log_total, row_delta = lax.map(query_block, jnp.arange(NBLK, dtype=jnp.int32))
    query_padded = jnp.pad(queries, ((WIN * BLK, WIN * BLK), (0, 0)))
    grad_padded = jnp.pad(grad_out, ((WIN * BLK, WIN * BLK), (0, 0)))
    log_padded = jnp.pad(log_total, ((WIN, WIN), (0, 0), (0, 0)))
    delta_padded = jnp.pad(row_delta, ((WIN, WIN), (0, 0), (0, 0)))

    def key_block(block_id):
        key_rows = lax.dynamic_slice_in_dim(kv_padded, (block_id + WIN) * BLK, BLK, 0).astype(jnp.float32).reshape(BLK, 2, H, DH)
        query_rows = lax.dynamic_slice_in_dim(query_padded, block_id * BLK, window_span * BLK, 0)
        query_rows = query_rows.astype(jnp.float32).reshape(window_span, BLK, H, DH)
        grad_rows = lax.dynamic_slice_in_dim(grad_padded, block_id * BLK, window_span * BLK, 0)
        grad_rows = grad_rows.astype(jnp.float32).reshape(window_span, BLK, H, DH)
        log_rows = lax.dynamic_slice_in_dim(log_padded, block_id, window_span, 0)
        delta_rows = lax.dynamic_slice_in_dim(delta_padded, block_id, window_span, 0)
        neighbour = block_id + jnp.arange(window_span, dtype=jnp.int32) - WIN
        inside = (neighbour >= 0) & (neighbour < NBLK)
        scores = jnp.einsum('uihe,jhe->uhij', query_rows, key_rows[:, 0], precision=highest) * score_scale
        weights = jnp.where(inside[:, None, None, None], jnp.exp(scores - log_rows[..., None]), 0.0)
        weights_low = lax.optimization_barrier(weights.astype(jnp.bfloat16)).astype(jnp.float32)
        grad_probs = jnp.einsum('uihe,jhe->uhij', grad_rows, key_rows[:, 1], precision=highest)
        grad_scores = weights * (grad_probs - delta_rows[..., None])
        grad_low = lax.optimization_barrier(grad_scores.astype(jnp.bfloat16)).astype(jnp.float32)
        key_grad = jnp.einsum('uhij,uihe->jhe', grad_low, query_rows, precision=highest) * score_scale
        value_grad = jnp.einsum('uhij,uihe->jhe', weights_low, grad_rows, precision=highest)
        return jnp.stack([key_grad, value_grad], axis=1).astype(jnp.bfloat16)
    kv_grads = lax.map(key_block, jnp.arange(NBLK, dtype=jnp.int32))
    return (attended.reshape(TOKENS, D), grad_query.reshape(TOKENS, D), kv_grads.reshape(TOKENS, 2, D))
```

```python
import functools
import math

import jax
import jax.numpy as jnp
from jax import lax
from jax.experimental import pallas as pl
from jax.experimental.pallas import tpu as pltpu
from jax.sharding import PartitionSpec as P

H = 8
DH = 128
D = H * DH
BLK = 64
WIN = 2
MEM = 4
PAIR = 2 * BLK
HALO = WIN * BLK
SPAN = PAIR + 2 * HALO
NEG_FILL = -1e30
SCALE = 1.0 / math.sqrt(DH)
EXP2_SCALE = SCALE * math.log2(math.e)

NT = (((1,), (1,)), ((), ()))
NN = (((1,), (0,)), ((), ()))
TN = (((0,), (0,)), ((), ()))


def dot(a, b, dims):
    return lax.dot_general(a, b, dims, preferred_element_type=jnp.float32)


def attention_kernel(
    slot_ref, edge_ref, q_ref, do_ref, left_ref, own_ref, right_ref, table_ref,
    att_ref, dq_ref, dkv_ref,
    kv, acc, sems, *, pairs,
):
    step = pl.program_id(0)

    @pl.when(step == 0)
    def _():
        rows = own_ref.shape[0]
        copies = [
            pltpu.make_async_copy(left_ref, kv.at[pl.ds(0, HALO)], sems.at[0]),
            pltpu.make_async_copy(own_ref, kv.at[pl.ds(HALO, rows)], sems.at[1]),
            pltpu.make_async_copy(right_ref, kv.at[pl.ds(HALO + rows, HALO)], sems.at[2]),
        ]
        for copy in copies:
            copy.start()
        acc[pl.ds(0, SPAN - PAIR), :] = jnp.zeros((SPAN - PAIR, 2 * D), jnp.float32)
        for copy in copies:
            copy.wait()

    @pl.when(step < pairs)
    def _():
        base = pl.multiple_of(step * PAIR, PAIR)
        window = pl.ds(base, SPAN)
        row = lax.broadcasted_iota(jnp.int32, (PAIR, PAIR), 0)
        lane = lax.broadcasted_iota(jnp.int32, (PAIR, PAIR), 1)
        no_left = jnp.logical_and(step == 0, edge_ref[0] == 1)
        no_right = jnp.logical_and(step == pairs - 1, edge_ref[1] == 1)
        bias_left = jnp.where(
            jnp.logical_and(jnp.logical_or(row < BLK, lane >= BLK), jnp.logical_not(no_left)),
            0.0, NEG_FILL,
        )
        bias_right = jnp.where(
            jnp.logical_and(jnp.logical_or(row >= BLK, lane < BLK), jnp.logical_not(no_right)),
            0.0, NEG_FILL,
        )

        mem_keys, mem_values = [], []
        for b in range(2):
            parts = [table_ref[slot_ref[(step * 2 + b) * MEM + m]] for m in range(MEM)]
            rows = jnp.concatenate(parts, axis=0)
            mem_keys.append(rows[:, :DH])
            mem_values.append(rows[:, DH:])

        def cols(h):
            return slice(h * DH, (h + 1) * DH)

        def stack(per_head):
            return [
                jnp.concatenate([x[b * BLK : (b + 1) * BLK] for x in per_head], axis=0)
                for b in range(2)
            ]

        def unstack(stacked, h):
            return jnp.concatenate([s[h * BLK : (h + 1) * BLK] for s in stacked], axis=0)

        q = [q_ref[:, cols(h)] for h in range(H)]
        mem_scores = [dot(x, k, NT) for x, k in zip(stack(q), mem_keys)]
        e_win, e_mem, p_win, p_mem, totals, out_win = [], [], [], [], [], []
        for h in range(H):
            sw = dot(q[h], kv[window, cols(h)], NT)
            sw = jnp.concatenate(
                [sw[:, :PAIR] + bias_left, sw[:, PAIR : 2 * PAIR], sw[:, 2 * PAIR :] + bias_right],
                axis=1,
            )
            sm = unstack(mem_scores, h)
            top = jnp.maximum(
                jnp.max(sw, axis=1, keepdims=True), jnp.max(sm, axis=1, keepdims=True)
            )
            ew = jnp.exp2((sw - top) * EXP2_SCALE)
            em = jnp.exp2((sm - top) * EXP2_SCALE)
            totals.append(jnp.sum(ew, axis=1, keepdims=True) + jnp.sum(em, axis=1, keepdims=True))
            e_win.append(ew)
            e_mem.append(em)
            p_win.append(ew.astype(jnp.bfloat16))
            p_mem.append(em.astype(jnp.bfloat16))
            out_win.append(dot(p_win[h], kv[window, slice(D + h * DH, D + (h + 1) * DH)], NN))
        out_mem = [dot(x, v, NN) for x, v in zip(stack(p_mem), mem_values)]
        scaled, deltas = [], []
        for h in range(H):
            inverse = 1.0 / totals[h]
            out = (out_win[h] + unstack(out_mem, h)) * inverse
            att_ref[:, cols(h)] = out.astype(jnp.bfloat16)
            low = (do_ref[:, cols(h)].astype(jnp.float32) * inverse).astype(jnp.bfloat16)
            scaled.append(low)
            deltas.append(jnp.sum(low.astype(jnp.float32) * out, axis=1, keepdims=True))
        mem_probs = [dot(x, v, NT) for x, v in zip(stack(scaled), mem_values)]
        ds_mem, dq_win = [], []
        for h in range(H):
            vcols = slice(D + h * DH, D + (h + 1) * DH)
            pw = dot(scaled[h], kv[window, vcols], NT)
            dsw = (e_win[h] * (pw - deltas[h])).astype(jnp.bfloat16)
            ds_mem.append((e_mem[h] * (unstack(mem_probs, h) - deltas[h])).astype(jnp.bfloat16))
            dq_win.append(dot(dsw, kv[window, cols(h)], NN))
            for columns, low, rows in ((cols(h), dsw, q[h]), (vcols, p_win[h], scaled[h])):
                term = dot(low, rows, TN)
                acc[pl.ds(base, SPAN - PAIR), columns] += term[: SPAN - PAIR]
                acc[pl.ds(base + SPAN - PAIR, PAIR), columns] = term[SPAN - PAIR :]
        dq_mem = [dot(x, k, NN) for x, k in zip(stack(ds_mem), mem_keys)]
        for h in range(H):
            dq_ref[:, cols(h)] = ((dq_win[h] + unstack(dq_mem, h)) * SCALE).astype(jnp.bfloat16)

    done = pl.ds(pl.multiple_of(step * PAIR, PAIR), PAIR)
    dkv_ref[:, :D] = (acc[done, :D] * SCALE).astype(jnp.bfloat16)
    dkv_ref[:, D:] = acc[done, D:].astype(jnp.bfloat16)


def attention(slots, edges, queries, grad_out, left, own, right, table):
    rows = queries.shape[0]
    pairs = rows // PAIR
    steps = pairs + 2 * HALO // PAIR
    ext = rows + 2 * HALO
    by_pair = pl.BlockSpec((PAIR, D), lambda i, *_: (jnp.minimum(i, pairs - 1), 0))
    spec = pltpu.PrefetchScalarGridSpec(
        num_scalar_prefetch=2,
        grid=(steps,),
        in_specs=[
            by_pair,
            by_pair,
            pl.BlockSpec(memory_space=pl.ANY),
            pl.BlockSpec(memory_space=pl.ANY),
            pl.BlockSpec(memory_space=pl.ANY),
            pl.BlockSpec(table.shape, lambda i, *_: (0, 0, 0), pipeline_mode=pl.Buffered(1)),
        ],
        out_specs=[
            by_pair,
            by_pair,
            pl.BlockSpec((PAIR, 2 * D), lambda i, *_: (i, 0)),
        ],
        scratch_shapes=[
            pltpu.VMEM((ext, 2 * D), jnp.bfloat16),
            pltpu.VMEM((ext, 2 * D), jnp.float32),
            pltpu.SemaphoreType.DMA((3,)),
        ],
    )
    return pl.pallas_call(
        functools.partial(attention_kernel, pairs=pairs),
        grid_spec=spec,
        out_shape=[
            jax.ShapeDtypeStruct((rows, D), jnp.bfloat16),
            jax.ShapeDtypeStruct((rows, D), jnp.bfloat16),
            jax.ShapeDtypeStruct((ext, 2 * D), jnp.bfloat16),
        ],
        compiler_params=pltpu.CompilerParams(vmem_limit_bytes=56 * 2**20),
        name="attention",
    )(slots, edges, queries, grad_out, left, own, right, table)


def per_device(queries, keys_values, memory, block_regions, region_slot, grad_out):
    rows = queries.shape[0]
    size = lax.axis_size("seq")
    me = lax.axis_index("seq")
    up = [(i, i + 1) for i in range(size - 1)]
    down = [(j, i) for i, j in up]
    left = lax.ppermute(keys_values[rows - HALO :].reshape(HALO, 2 * D), "seq", up)
    right = lax.ppermute(keys_values[:HALO].reshape(HALO, 2 * D), "seq", down)
    table = lax.all_gather(memory, "seq", axis=0, tiled=True)
    slots = region_slot[block_regions.reshape(-1)]
    edges = jnp.stack([me == 0, me == size - 1]).astype(jnp.int32)
    own = keys_values.reshape(rows, 2 * D)
    attended, grad_queries, grads = attention(
        slots, edges, queries, grad_out, left, own, right, table
    )
    from_right = lax.ppermute(grads[:HALO], "seq", down)
    from_left = lax.ppermute(grads[HALO + rows :], "seq", up)
    kept = grads[HALO : HALO + rows].astype(jnp.float32)
    kept = jnp.concatenate(
        [
            kept[:HALO] + from_left.astype(jnp.float32),
            kept[HALO : rows - HALO],
            kept[rows - HALO :] + from_right.astype(jnp.float32),
        ],
        axis=0,
    )
    return attended, grad_queries, kept.astype(jnp.bfloat16).reshape(rows, 2, D)


def solution(mesh):
    placed = (
        P("seq", None),
        P("seq", None, None),
        P("seq", None, None),
        P("seq", None),
        P(),
        P("seq", None),
    )
    return jax.shard_map(
        per_device,
        mesh=mesh,
        in_specs=placed,
        out_specs=(P("seq", None), P("seq", None), P("seq", None, None)),
        check_vma=False,
    )
```

```python
import functools
import math

import jax
import jax.numpy as jnp
from jax import lax
from jax.experimental import pallas as pl
from jax.experimental.pallas import tpu as pltpu
from jax.sharding import PartitionSpec as P

H = 8
DH = 128
D = H * DH
BLK = 64
WIN = 2
MEM = 4
PAIR = 2 * BLK
HALO = WIN * BLK
SPAN = PAIR + 2 * HALO
NEG_FILL = -1e30
SCALE = 1.0 / math.sqrt(DH)
EXP2_SCALE = SCALE * math.log2(math.e)

MESH = pl.DeviceIdType.MESH

NT = (((1,), (1,)), ((), ()))
NN = (((1,), (0,)), ((), ()))
TN = (((0,), (0,)), ((), ()))


def dot(a, b, dims):
    return lax.dot_general(a, b, dims, preferred_element_type=jnp.float32)


def flipped(number, mask):
    for bit in (1, 2, 4, 8, 16):
        if mask & bit:
            number = number + bit - 2 * bit * (number // bit % 2)
    return number


CORE, X, Y, Z, ZZ = 1, 2, 4, 8, 24
COLUMN = (0, Z, ZZ, Z ^ ZZ)


def gather_steps():
    steps = [(0, None, (Z, ZZ, X, Y, CORE))]
    steps += [(Z, None, (X, Y, CORE)), (ZZ, None, (Z, X, Y, CORE))]
    steps += [(X, None, ()), (Y, None, ()), (Z ^ ZZ, None, (X, Y, CORE))]
    steps += [(side ^ k, None, ()) for k in COLUMN[1:] for side in (X, Y)]
    steps += [(X ^ Y ^ k, half, (CORE,)) for k in COLUMN for half in (0, 1)]
    return steps


def sends():
    groups = []
    for block, half, partners in gather_steps():
        group = [(block, half, partner) for partner in partners]
        if block in [X ^ k for k in COLUMN]:
            group = [(block, 0, Y), (block, None, CORE)]
        if block in [Y ^ k for k in COLUMN]:
            group = [(block, 1, X), (block, None, CORE)]
        groups.append((block, half, group))
    return groups


def exchange_kernel(mem_ref, own_ref, table_ref, left_ref, right_ref, local_sem, send_sems, recv_sems, halo_sems, *, size, gather):
    me = lax.axis_index("seq")
    after, before = lax.rem(me + 1, size), lax.rem(me + size - 1, size)
    masks = (CORE, X, Y, Z, ZZ) if gather else ()
    barrier = pltpu.get_barrier_semaphore()
    partners = [flipped(me, mask) for mask in masks] + [after, before]
    for partner in partners:
        pl.semaphore_signal(barrier, inc=1, device_id=(partner,), device_id_type=MESH)
    pl.semaphore_wait(barrier, len(partners))

    rows = own_ref.shape[0]
    halos = [
        pltpu.make_async_remote_copy(
            src_ref=own_ref.at[pl.ds(start, HALO)], dst_ref=dst,
            send_sem=halo_sems.at[2 * i], recv_sem=halo_sems.at[2 * i + 1],
            device_id=(target,), device_id_type=MESH,
        )
        for i, (start, dst, target) in enumerate(
            ((rows - HALO, left_ref, after), (0, right_ref, before))
        )
    ]
    if not gather:
        for halo in halos:
            halo.start()
        for halo in halos:
            halo.wait()
        return
    blocks = mem_ref.shape[0]

    def part(half):
        return (0, blocks) if half is None else (half * (blocks // 2), blocks // 2)

    def slot(block, half):
        start, length = part(half)
        return table_ref.at[pl.ds(flipped(me, block) * blocks + start, length)]

    def copy(block, half, partner, number):
        start, length = part(half)
        target = slot(block, half)
        return pltpu.make_async_remote_copy(
            src_ref=mem_ref.at[pl.ds(start, length)] if block == 0 else target,
            dst_ref=target,
            send_sem=send_sems.at[number],
            recv_sem=recv_sems.at[2 * (block ^ partner) + (half or 0)],
            device_id=(flipped(me, partner),), device_id_type=MESH,
        )

    def arrived(block, half):
        target = slot(block, half)
        pltpu.make_async_remote_copy(
            src_ref=target, dst_ref=target, send_sem=send_sems.at[0],
            recv_sem=recv_sems.at[2 * block + (half or 0)],
            device_id=(flipped(me, CORE),), device_id_type=MESH,
        ).wait_recv()

    kept = pltpu.make_async_copy(mem_ref, slot(0, None), local_sem)
    kept.start()
    started = []
    for block, half, group in sends():
        if block:
            arrived(block, half)
        for b, h, partner in group:
            started.append(copy(b, h, partner, len(started)))
            started[-1].start()
        if block == 0:
            for halo in halos:
                halo.start()
    for block, half, group in sends():
        arrived(block ^ CORE, half)
    for one in started:
        one.wait_send()
    kept.wait()
    for halo in halos:
        halo.wait()


def exchange(memory, own, size, gather):
    count = sum(len(group) for _, _, group in sends())
    whole = memory.shape[0] * (size if gather else 1)
    anywhere = pl.BlockSpec(memory_space=pl.ANY)
    return pl.pallas_call(
        functools.partial(exchange_kernel, size=size, gather=gather),
        in_specs=[anywhere] * 2,
        out_specs=[anywhere] * 3,
        out_shape=[
            jax.ShapeDtypeStruct((whole,) + memory.shape[1:], memory.dtype),
            jax.ShapeDtypeStruct((HALO, 2 * D), own.dtype),
            jax.ShapeDtypeStruct((HALO, 2 * D), own.dtype),
        ],
        scratch_shapes=[
            pltpu.SemaphoreType.DMA,
            pltpu.SemaphoreType.DMA((count,)),
            pltpu.SemaphoreType.DMA((64,)),
            pltpu.SemaphoreType.DMA((4,)),
        ],
        compiler_params=pltpu.CompilerParams(collective_id=0, has_side_effects=True),
        name="exchange",
    )(memory, own)


def attention_kernel(
    slot_ref, edge_ref, q_ref, do_ref, left_ref, own_ref, right_ref, table_ref,
    att_ref, dq_ref, dleft_ref, dkv_ref, dright_ref,
    kv, acc, sems, *, pairs,
):
    step = pl.program_id(0)

    @pl.when(step == 0)
    def _():
        rows = own_ref.shape[0]
        copies = [
            pltpu.make_async_copy(left_ref, kv.at[pl.ds(0, HALO)], sems.at[0]),
            pltpu.make_async_copy(own_ref, kv.at[pl.ds(HALO, rows)], sems.at[1]),
            pltpu.make_async_copy(right_ref, kv.at[pl.ds(HALO + rows, HALO)], sems.at[2]),
        ]
        for copy in copies:
            copy.start()
        acc[pl.ds(0, SPAN - PAIR), :] = jnp.zeros((SPAN - PAIR, 2 * D), jnp.float32)
        for copy in copies:
            copy.wait()

    @pl.when(step < pairs)
    def _():
        base = pl.multiple_of(step * PAIR, PAIR)
        window = pl.ds(base, SPAN)
        row = lax.broadcasted_iota(jnp.int32, (PAIR, PAIR), 0)
        lane = lax.broadcasted_iota(jnp.int32, (PAIR, PAIR), 1)
        no_left = jnp.logical_and(step == 0, edge_ref[0] == 1)
        no_right = jnp.logical_and(step == pairs - 1, edge_ref[1] == 1)
        bias_left = jnp.where(
            jnp.logical_and(jnp.logical_or(row < BLK, lane >= BLK), jnp.logical_not(no_left)),
            0.0, NEG_FILL,
        )
        bias_right = jnp.where(
            jnp.logical_and(jnp.logical_or(row >= BLK, lane < BLK), jnp.logical_not(no_right)),
            0.0, NEG_FILL,
        )

        mem_keys, mem_values = [], []
        for b in range(2):
            parts = [table_ref[slot_ref[(step * 2 + b) * MEM + m]] for m in range(MEM)]
            rows = jnp.concatenate(parts, axis=0)
            mem_keys.append(rows[:, :DH])
            mem_values.append(rows[:, DH:])

        def cols(h):
            return slice(h * DH, (h + 1) * DH)

        def stack(per_head):
            return [
                jnp.concatenate([x[b * BLK : (b + 1) * BLK] for x in per_head], axis=0)
                for b in range(2)
            ]

        def unstack(stacked, h):
            return jnp.concatenate([s[h * BLK : (h + 1) * BLK] for s in stacked], axis=0)

        q = [q_ref[:, cols(h)] for h in range(H)]
        mem_scores = [dot(x, k, NT) for x, k in zip(stack(q), mem_keys)]
        e_win, e_mem, p_win, p_mem, totals, out_win = [], [], [], [], [], []
        for h in range(H):
            sw = dot(q[h], kv[window, cols(h)], NT)
            sw = jnp.concatenate(
                [sw[:, :PAIR] + bias_left, sw[:, PAIR : 2 * PAIR], sw[:, 2 * PAIR :] + bias_right],
                axis=1,
            )
            sm = unstack(mem_scores, h)
            top = jnp.maximum(
                jnp.max(sw, axis=1, keepdims=True), jnp.max(sm, axis=1, keepdims=True)
            )
            ew = jnp.exp2((sw - top) * EXP2_SCALE)
            em = jnp.exp2((sm - top) * EXP2_SCALE)
            totals.append(jnp.sum(ew, axis=1, keepdims=True) + jnp.sum(em, axis=1, keepdims=True))
            e_win.append(ew)
            e_mem.append(em)
            p_win.append(ew.astype(jnp.bfloat16))
            p_mem.append(em.astype(jnp.bfloat16))
            out_win.append(dot(p_win[h], kv[window, slice(D + h * DH, D + (h + 1) * DH)], NN))
        out_mem = [dot(x, v, NN) for x, v in zip(stack(p_mem), mem_values)]
        scaled, deltas = [], []
        for h in range(H):
            inverse = 1.0 / totals[h]
            out = (out_win[h] + unstack(out_mem, h)) * inverse
            att_ref[:, cols(h)] = out.astype(jnp.bfloat16)
            low = (do_ref[:, cols(h)].astype(jnp.float32) * inverse).astype(jnp.bfloat16)
            scaled.append(low)
            deltas.append(jnp.sum(low.astype(jnp.float32) * out, axis=1, keepdims=True))
        mem_probs = [dot(x, v, NT) for x, v in zip(stack(scaled), mem_values)]
        ds_mem, dq_win = [], []
        for h in range(H):
            vcols = slice(D + h * DH, D + (h + 1) * DH)
            pw = dot(scaled[h], kv[window, vcols], NT)
            dsw = (e_win[h] * (pw - deltas[h])).astype(jnp.bfloat16)
            ds_mem.append((e_mem[h] * (unstack(mem_probs, h) - deltas[h])).astype(jnp.bfloat16))
            dq_win.append(dot(dsw, kv[window, cols(h)], NN))
            for columns, low, rows in ((cols(h), dsw, q[h]), (vcols, p_win[h], scaled[h])):
                term = dot(low, rows, TN)
                acc[pl.ds(base, SPAN - PAIR), columns] += term[: SPAN - PAIR]
                acc[pl.ds(base + SPAN - PAIR, PAIR), columns] = term[SPAN - PAIR :]
        dq_mem = [dot(x, k, NN) for x, k in zip(stack(ds_mem), mem_keys)]
        for h in range(H):
            dq_ref[:, cols(h)] = ((dq_win[h] + unstack(dq_mem, h)) * SCALE).astype(jnp.bfloat16)

    done = pl.ds(pl.multiple_of(step * PAIR, PAIR), PAIR)
    finished = jnp.concatenate(
        [(acc[done, :D] * SCALE).astype(jnp.bfloat16), acc[done, D:].astype(jnp.bfloat16)], axis=1
    )

    @pl.when(step == 0)
    def _():
        dleft_ref[...] = finished

    @pl.when(jnp.logical_and(step > 0, step <= pairs))
    def _():
        dkv_ref[...] = finished

    @pl.when(step == pairs + 1)
    def _():
        dright_ref[...] = finished


def attention(slots, edges, queries, grad_out, left, own, right, table):
    rows = queries.shape[0]
    pairs = rows // PAIR
    steps = pairs + 2 * HALO // PAIR
    ext = rows + 2 * HALO
    by_pair = pl.BlockSpec((PAIR, D), lambda i, *_: (jnp.minimum(i, pairs - 1), 0))
    spec = pltpu.PrefetchScalarGridSpec(
        num_scalar_prefetch=2,
        grid=(steps,),
        in_specs=[
            by_pair,
            by_pair,
            pl.BlockSpec(memory_space=pl.ANY),
            pl.BlockSpec(memory_space=pl.ANY),
            pl.BlockSpec(memory_space=pl.ANY),
            pl.BlockSpec(table.shape, lambda i, *_: (0, 0, 0), pipeline_mode=pl.Buffered(1)),
        ],
        out_specs=[
            by_pair,
            by_pair,
            pl.BlockSpec((HALO, 2 * D), lambda i, *_: (0, 0)),
            pl.BlockSpec((PAIR, 2 * D), lambda i, *_: (jnp.clip(i - 1, 0, pairs - 1), 0)),
            pl.BlockSpec((HALO, 2 * D), lambda i, *_: (0, 0)),
        ],
        scratch_shapes=[
            pltpu.VMEM((ext, 2 * D), jnp.bfloat16),
            pltpu.VMEM((ext, 2 * D), jnp.float32),
            pltpu.SemaphoreType.DMA((3,)),
        ],
    )
    return pl.pallas_call(
        functools.partial(attention_kernel, pairs=pairs),
        grid_spec=spec,
        out_shape=[
            jax.ShapeDtypeStruct((rows, D), jnp.bfloat16),
            jax.ShapeDtypeStruct((rows, D), jnp.bfloat16),
            jax.ShapeDtypeStruct((HALO, 2 * D), jnp.bfloat16),
            jax.ShapeDtypeStruct((rows, 2 * D), jnp.bfloat16),
            jax.ShapeDtypeStruct((HALO, 2 * D), jnp.bfloat16),
        ],
        compiler_params=pltpu.CompilerParams(vmem_limit_bytes=56 * 2**20),
        name="attention",
    )(slots, edges, queries, grad_out, left, own, right, table)


def per_device(queries, keys_values, memory, block_regions, region_slot, grad_out):
    rows = queries.shape[0]
    size = lax.axis_size("seq")
    me = lax.axis_index("seq")
    up = [(i, i + 1) for i in range(size - 1)]
    down = [(j, i) for i, j in up]
    own = keys_values.reshape(rows, 2 * D)
    gather = size == 32
    table, left, right = exchange(memory, own, size, gather)
    if not gather:
        table = lax.all_gather(memory, "seq", axis=0, tiled=True)
    slots = region_slot[block_regions.reshape(-1)]
    edges = jnp.stack([me == 0, me == size - 1]).astype(jnp.int32)
    attended, grad_queries, to_left, grads, to_right = attention(
        slots, edges, queries, grad_out, left, own, right, table
    )
    from_right = lax.ppermute(to_left, "seq", down)
    from_left = lax.ppermute(to_right, "seq", up)
    kept = lax.optimization_barrier(grads.reshape(rows, 2, D))
    for start, arrived in ((0, from_left), (rows - HALO, from_right)):
        total = kept[start : start + HALO].astype(jnp.float32) + arrived.reshape(
            HALO, 2, D
        ).astype(jnp.float32)
        kept = lax.dynamic_update_slice(kept, total.astype(jnp.bfloat16), (start, 0, 0))
    return attended, grad_queries, kept


def solution(mesh):
    placed = (
        P("seq", None),
        P("seq", None, None),
        P("seq", None, None),
        P("seq", None),
        P(),
        P("seq", None),
    )
    return jax.shard_map(
        per_device,
        mesh=mesh,
        in_specs=placed,
        out_specs=(P("seq", None), P("seq", None), P("seq", None, None)),
        check_vma=False,
    )
```

```python
import functools
import math

import jax
import jax.numpy as jnp
from jax import lax
from jax.experimental import pallas as pl
from jax.experimental.pallas import tpu as pltpu
from jax.sharding import PartitionSpec as P

H = 8
DH = 128
D = H * DH
BLK = 64
WIN = 2
MEM = 4
PAIR = 2 * BLK
HALO = WIN * BLK
SPAN = PAIR + 2 * HALO
NEG_FILL = -1e30
SCALE = 1.0 / math.sqrt(DH)
EXP2_SCALE = SCALE * math.log2(math.e)

MESH = pl.DeviceIdType.MESH

NT = (((1,), (1,)), ((), ()))
NN = (((1,), (0,)), ((), ()))
TN = (((0,), (0,)), ((), ()))


def dot(a, b, dims):
    return lax.dot_general(a, b, dims, preferred_element_type=jnp.float32)


def flipped(number, mask):
    for bit in (1, 2, 4, 8, 16):
        if mask & bit:
            number = number + bit - 2 * bit * (number // bit % 2)
    return number


CORE, X, Y, Z, ZZ = 1, 2, 4, 8, 24
COLUMN = (0, Z, ZZ, Z ^ ZZ)


def gather_steps():
    steps = [(0, None, (Z, ZZ, X, Y, CORE))]
    steps += [(Z, None, (X, Y, CORE)), (ZZ, None, (Z, X, Y, CORE))]
    steps += [(X, None, ()), (Y, None, ()), (Z ^ ZZ, None, (X, Y, CORE))]
    steps += [(side ^ k, None, ()) for k in COLUMN[1:] for side in (X, Y)]
    steps += [(X ^ Y ^ k, half, (CORE,)) for k in COLUMN for half in (0, 1)]
    return steps


def sends():
    groups = []
    for block, half, partners in gather_steps():
        group = [(block, half, partner) for partner in partners]
        if block in [X ^ k for k in COLUMN]:
            group = [(block, 0, Y), (block, None, CORE)]
        if block in [Y ^ k for k in COLUMN]:
            group = [(block, 1, X), (block, None, CORE)]
        groups.append((block, half, group))
    return groups


def exchange_kernel(
    mem_ref, own_ref, q_ref, do_ref,
    table_ref, left_ref, right_ref, e_ref, dp_ref, out_ref, stat_ref,
    kv, q, do, e_own, dp_own, out_own, stat_own,
    local_sem, send_sems, recv_sems, halo_sems, load_sems, store_sems, *, size, gather,
):
    me = lax.axis_index("seq")
    after, before = lax.rem(me + 1, size), lax.rem(me + size - 1, size)
    masks = (CORE, X, Y, Z, ZZ) if gather else ()
    barrier = pltpu.get_barrier_semaphore()
    partners = [flipped(me, mask) for mask in masks] + [after, before]
    for partner in partners:
        pl.semaphore_signal(barrier, inc=1, device_id=(partner,), device_id_type=MESH)
    pl.semaphore_wait(barrier, len(partners))

    rows = own_ref.shape[0]
    halos = [
        pltpu.make_async_remote_copy(
            src_ref=own_ref.at[pl.ds(start, HALO)], dst_ref=dst,
            send_sem=halo_sems.at[2 * i], recv_sem=halo_sems.at[2 * i + 1],
            device_id=(target,), device_id_type=MESH,
        )
        for i, (start, dst, target) in enumerate(
            ((rows - HALO, left_ref, after), (0, right_ref, before))
        )
    ]
    blocks = mem_ref.shape[0]

    def part(half):
        return (0, blocks) if half is None else (half * (blocks // 2), blocks // 2)

    def slot(block, half):
        start, length = part(half)
        return table_ref.at[pl.ds(flipped(me, block) * blocks + start, length)]

    def copy(block, half, partner, number):
        start, length = part(half)
        target = slot(block, half)
        return pltpu.make_async_remote_copy(
            src_ref=mem_ref.at[pl.ds(start, length)] if block == 0 else target,
            dst_ref=target,
            send_sem=send_sems.at[number],
            recv_sem=recv_sems.at[2 * (block ^ partner) + (half or 0)],
            device_id=(flipped(me, partner),), device_id_type=MESH,
        )

    def arrived(block, half):
        target = slot(block, half)
        pltpu.make_async_remote_copy(
            src_ref=target, dst_ref=target, send_sem=send_sems.at[0],
            recv_sem=recv_sems.at[2 * block + (half or 0)],
            device_id=(flipped(me, CORE),), device_id_type=MESH,
        ).wait_recv()

    groups = sends() if gather else []
    started = []

    def forward(first, last):
        for block, half, group in groups[first:last]:
            if block:
                arrived(block, half)
            for b, h, partner in group:
                started.append(copy(b, h, partner, len(started)))
                started[-1].start()

    pairs = rows // PAIR
    row = lax.broadcasted_iota(jnp.int32, (PAIR, PAIR), 0)
    lane = lax.broadcasted_iota(jnp.int32, (PAIR, PAIR), 1)
    stores = []

    def window_part(p):
        see_left = jnp.logical_or(row < BLK, lane >= BLK)
        see_right = jnp.logical_or(row >= BLK, lane < BLK)
        if p == 0:
            see_left = jnp.logical_and(see_left, me > 0)
        if p == pairs - 1:
            see_right = jnp.logical_and(see_right, me < size - 1)
        bias_left = jnp.where(see_left, 0.0, NEG_FILL)
        bias_right = jnp.where(see_right, 0.0, NEG_FILL)
        mine = pl.ds(p * PAIR, PAIR)
        window = pl.ds(p * PAIR, SPAN)

        def head(h, carry):
            columns = pl.ds(pl.multiple_of(h * DH, DH), DH)
            wide = pl.ds(pl.multiple_of(h * SPAN, DH), SPAN)
            values = kv[window, pl.ds(pl.multiple_of(D + h * DH, DH), DH)]
            sw = dot(q[mine, columns], kv[window, columns], NT)
            dp_own[mine, wide] = dot(do[mine, columns], values, NT)
            sw = jnp.concatenate(
                [sw[:, :PAIR] + bias_left, sw[:, PAIR : 2 * PAIR], sw[:, 2 * PAIR :] + bias_right],
                axis=1,
            )
            top = jnp.max(sw, axis=1, keepdims=True)
            ew = jnp.exp2((sw - top) * EXP2_SCALE)
            e_own[mine, wide] = ew
            total = jnp.sum(ew, axis=1, keepdims=True)
            stat_own[mine, columns] = jnp.where(lane < BLK, top, total)
            out_own[mine, columns] = dot(ew.astype(jnp.bfloat16), values, NN)
            return carry

        lax.fori_loop(0, H, head, 0, unroll=2)
        for src, dst in ((e_own, e_ref), (dp_own, dp_ref), (out_own, out_ref), (stat_own, stat_ref)):
            stores.append(
                pltpu.make_async_copy(src.at[mine], dst.at[mine], store_sems.at[len(stores)])
            )
            stores[-1].start()

    forward(0, 1)
    for halo in halos:
        halo.start()
    loads = [
        pltpu.make_async_copy(src, dst, load_sems.at[i])
        for i, (src, dst) in enumerate((
            (own_ref, kv.at[pl.ds(HALO, rows)]), (q_ref, q), (do_ref, do),
            (left_ref, kv.at[pl.ds(0, HALO)]), (right_ref, kv.at[pl.ds(HALO + rows, HALO)]),
        ))
    ]
    for load in loads[:3]:
        load.start()
    if gather:
        kept = pltpu.make_async_copy(mem_ref, slot(0, None), local_sem)
        kept.start()
    for load in loads[:3]:
        load.wait()
    window_part(1)
    forward(1, 3)
    window_part(2)
    forward(3, 6)
    window_part(3)
    forward(6, 8)
    for p in range(4, pairs - 2):
        window_part(p)
    forward(8, 10)
    for halo in halos:
        halo.wait()
    for load in loads[3:]:
        load.start()
    window_part(pairs - 2)
    for load in loads[3:]:
        load.wait()
    forward(10, 12)
    window_part(0)
    forward(12, 14)
    window_part(pairs - 1)
    forward(14, len(groups))
    for block, half, group in groups:
        arrived(block ^ CORE, half)
    for one in started:
        one.wait_send()
    if gather:
        kept.wait()
    for store in stores:
        store.wait()


def exchange(memory, own, queries, grad_out, size, gather):
    count = sum(len(group) for _, _, group in sends())
    rows = own.shape[0]
    whole = memory.shape[0] * (size if gather else 1)
    anywhere = pl.BlockSpec(memory_space=pl.ANY)
    made = [
        (rows, H * SPAN),
        (rows, H * SPAN),
        (rows, D),
        (rows, D),
    ]
    return pl.pallas_call(
        functools.partial(exchange_kernel, size=size, gather=gather),
        in_specs=[anywhere] * 4,
        out_specs=[anywhere] * 7,
        out_shape=[
            jax.ShapeDtypeStruct((whole,) + memory.shape[1:], memory.dtype),
            jax.ShapeDtypeStruct((HALO, 2 * D), own.dtype),
            jax.ShapeDtypeStruct((HALO, 2 * D), own.dtype),
        ] + [jax.ShapeDtypeStruct(shape, jnp.float32) for shape in made],
        scratch_shapes=[
            pltpu.VMEM((rows + 2 * HALO, 2 * D), jnp.bfloat16),
            pltpu.VMEM((rows, D), jnp.bfloat16),
            pltpu.VMEM((rows, D), jnp.bfloat16),
        ] + [pltpu.VMEM(shape, jnp.float32) for shape in made] + [
            pltpu.SemaphoreType.DMA,
            pltpu.SemaphoreType.DMA((count,)),
            pltpu.SemaphoreType.DMA((64,)),
            pltpu.SemaphoreType.DMA((4,)),
            pltpu.SemaphoreType.DMA((5,)),
            pltpu.SemaphoreType.DMA((4 * rows // PAIR,)),
        ],
        compiler_params=pltpu.CompilerParams(
            collective_id=0, has_side_effects=True, vmem_limit_bytes=56 * 2**20
        ),
        name="exchange",
    )(memory, own, queries, grad_out)


def attention_kernel(
    slot_ref, q_ref, do_ref, e_ref, dp_ref, out_ref, stat_ref, left_ref, own_ref, right_ref, table_ref,
    att_ref, dq_ref, dleft_ref, dkv_ref, dright_ref,
    keys, acc, sems, *, pairs,
):
    step = pl.program_id(0)

    @pl.when(step == 0)
    def _():
        rows = own_ref.shape[0]
        half = pl.ds(0, D)
        copies = [
            pltpu.make_async_copy(left_ref.at[:, half], keys.at[pl.ds(0, HALO)], sems.at[0]),
            pltpu.make_async_copy(own_ref.at[:, half], keys.at[pl.ds(HALO, rows)], sems.at[1]),
            pltpu.make_async_copy(right_ref.at[:, half], keys.at[pl.ds(HALO + rows, HALO)], sems.at[2]),
        ]
        for copy in copies:
            copy.start()
        acc[pl.ds(0, SPAN - PAIR), :] = jnp.zeros((SPAN - PAIR, 2 * D), jnp.float32)
        for copy in copies:
            copy.wait()

    @pl.when(step < pairs)
    def _():
        base = pl.multiple_of(step * PAIR, PAIR)
        window = pl.ds(base, SPAN)

        mem_keys, mem_values = [], []
        for b in range(2):
            parts = [table_ref[slot_ref[(step * 2 + b) * MEM + m]] for m in range(MEM)]
            rows = jnp.concatenate(parts, axis=0)
            mem_keys.append(rows[:, :DH])
            mem_values.append(rows[:, DH:])

        def cols(h):
            return slice(h * DH, (h + 1) * DH)

        def stack(per_head):
            return [
                jnp.concatenate([x[b * BLK : (b + 1) * BLK] for x in per_head], axis=0)
                for b in range(2)
            ]

        def unstack(stacked, h):
            return jnp.concatenate([s[h * BLK : (h + 1) * BLK] for s in stacked], axis=0)

        q = [q_ref[:, cols(h)] for h in range(H)]
        mem_scores = [dot(x, k, NT) for x, k in zip(stack(q), mem_keys)]
        e_mem, inverses, shares = [], [], []
        for h in range(H):
            sm = unstack(mem_scores, h)
            win_top = stat_ref[:, h * DH : h * DH + 1]
            win_total = stat_ref[:, h * DH + BLK : h * DH + BLK + 1]
            top = jnp.maximum(win_top, jnp.max(sm, axis=1, keepdims=True))
            em = jnp.exp2((sm - top) * EXP2_SCALE)
            share = jnp.exp2((win_top - top) * EXP2_SCALE)
            inverse = 1.0 / (share * win_total + jnp.sum(em, axis=1, keepdims=True))
            e_mem.append(em)
            inverses.append(inverse)
            shares.append(share * inverse)
        out_mem = [
            dot(x, v, NN)
            for x, v in zip(stack([em.astype(jnp.bfloat16) for em in e_mem]), mem_values)
        ]
        low_win, low_mem, deltas, mem_deltas = [], [], [], []
        for h in range(H):
            out = out_ref[:, cols(h)] * shares[h] + unstack(out_mem, h) * inverses[h]
            att_ref[:, cols(h)] = out.astype(jnp.bfloat16)
            grad = do_ref[:, cols(h)].astype(jnp.float32)
            low_win.append((grad * shares[h]).astype(jnp.bfloat16))
            low_mem.append((grad * inverses[h]).astype(jnp.bfloat16))
            deltas.append(jnp.sum(grad * out, axis=1, keepdims=True))
            mem_deltas.append(jnp.sum(low_mem[h].astype(jnp.float32) * out, axis=1, keepdims=True))
        mem_probs = [dot(x, v, NT) for x, v in zip(stack(low_mem), mem_values)]
        ds_mem, dq_win = [], []
        for h in range(H):
            wide = slice(h * SPAN, (h + 1) * SPAN)
            ew = e_ref[:, wide]
            dsw = ((ew * shares[h]) * (dp_ref[:, wide] - deltas[h])).astype(jnp.bfloat16)
            ds_mem.append((e_mem[h] * (unstack(mem_probs, h) - mem_deltas[h])).astype(jnp.bfloat16))
            dq_win.append(dot(dsw, keys[window, cols(h)], NN))
            vcols = slice(D + h * DH, D + (h + 1) * DH)
            for columns, low, rows in (
                (cols(h), dsw, q[h]),
                (vcols, ew.astype(jnp.bfloat16), low_win[h]),
            ):
                term = dot(low, rows, TN)
                acc[pl.ds(base, SPAN - PAIR), columns] += term[: SPAN - PAIR]
                acc[pl.ds(base + SPAN - PAIR, PAIR), columns] = term[SPAN - PAIR :]
        dq_mem = [dot(x, k, NN) for x, k in zip(stack(ds_mem), mem_keys)]
        for h in range(H):
            dq_ref[:, cols(h)] = ((dq_win[h] + unstack(dq_mem, h)) * SCALE).astype(jnp.bfloat16)

    done = pl.ds(pl.multiple_of(step * PAIR, PAIR), PAIR)
    finished = jnp.concatenate(
        [(acc[done, :D] * SCALE).astype(jnp.bfloat16), acc[done, D:].astype(jnp.bfloat16)], axis=1
    )

    @pl.when(step == 0)
    def _():
        dleft_ref[...] = finished

    @pl.when(jnp.logical_and(step > 0, step <= pairs))
    def _():
        dkv_ref[...] = finished

    @pl.when(step == pairs + 1)
    def _():
        dright_ref[...] = finished


def attention(slots, queries, grad_out, e, dp, out, stat, left, own, right, table):
    rows = queries.shape[0]
    pairs = rows // PAIR
    steps = pairs + 2 * HALO // PAIR
    ext = rows + 2 * HALO
    by_pair = pl.BlockSpec((PAIR, D), lambda i, *_: (jnp.minimum(i, pairs - 1), 0))
    wide = pl.BlockSpec((PAIR, H * SPAN), lambda i, *_: (jnp.minimum(i, pairs - 1), 0))
    spec = pltpu.PrefetchScalarGridSpec(
        num_scalar_prefetch=1,
        grid=(steps,),
        in_specs=[
            by_pair,
            by_pair,
            wide,
            wide,
            by_pair,
            by_pair,
            pl.BlockSpec(memory_space=pl.ANY),
            pl.BlockSpec(memory_space=pl.ANY),
            pl.BlockSpec(memory_space=pl.ANY),
            pl.BlockSpec(table.shape, lambda i, *_: (0, 0, 0), pipeline_mode=pl.Buffered(1)),
        ],
        out_specs=[
            by_pair,
            by_pair,
            pl.BlockSpec((HALO, 2 * D), lambda i, *_: (0, 0)),
            pl.BlockSpec((PAIR, 2 * D), lambda i, *_: (jnp.clip(i - 1, 0, pairs - 1), 0)),
            pl.BlockSpec((HALO, 2 * D), lambda i, *_: (0, 0)),
        ],
        scratch_shapes=[
            pltpu.VMEM((ext, D), jnp.bfloat16),
            pltpu.VMEM((ext, 2 * D), jnp.float32),
            pltpu.SemaphoreType.DMA((3,)),
        ],
    )
    return pl.pallas_call(
        functools.partial(attention_kernel, pairs=pairs),
        grid_spec=spec,
        out_shape=[
            jax.ShapeDtypeStruct((rows, D), jnp.bfloat16),
            jax.ShapeDtypeStruct((rows, D), jnp.bfloat16),
            jax.ShapeDtypeStruct((HALO, 2 * D), jnp.bfloat16),
            jax.ShapeDtypeStruct((rows, 2 * D), jnp.bfloat16),
            jax.ShapeDtypeStruct((HALO, 2 * D), jnp.bfloat16),
        ],
        compiler_params=pltpu.CompilerParams(vmem_limit_bytes=56 * 2**20),
        name="attention",
    )(slots, queries, grad_out, e, dp, out, stat, left, own, right, table)


def per_device(queries, keys_values, memory, block_regions, region_slot, grad_out):
    rows = queries.shape[0]
    size = lax.axis_size("seq")
    up = [(i, i + 1) for i in range(size - 1)]
    down = [(j, i) for i, j in up]
    own = keys_values.reshape(rows, 2 * D)
    gather = size == 32
    table, left, right, e, dp, out, stat = exchange(
        memory, own, queries, grad_out, size, gather
    )
    if not gather:
        table = lax.all_gather(memory, "seq", axis=0, tiled=True)
    slots = region_slot[block_regions.reshape(-1)]
    attended, grad_queries, to_left, grads, to_right = attention(
        slots, queries, grad_out, e, dp, out, stat, left, own, right, table
    )
    from_right = lax.ppermute(to_left, "seq", down)
    from_left = lax.ppermute(to_right, "seq", up)
    kept = lax.optimization_barrier(grads.reshape(rows, 2, D))
    for start, arrived in ((0, from_left), (rows - HALO, from_right)):
        total = kept[start : start + HALO].astype(jnp.float32) + arrived.reshape(
            HALO, 2, D
        ).astype(jnp.float32)
        kept = lax.dynamic_update_slice(kept, total.astype(jnp.bfloat16), (start, 0, 0))
    return attended, grad_queries, kept


def solution(mesh):
    placed = (
        P("seq", None),
        P("seq", None, None),
        P("seq", None, None),
        P("seq", None),
        P(),
        P("seq", None),
    )
    return jax.shard_map(
        per_device,
        mesh=mesh,
        in_specs=placed,
        out_specs=(P("seq", None), P("seq", None), P("seq", None, None)),
        check_vma=False,
    )
```

```python
import functools
import math

import jax
import jax.numpy as jnp
from jax import lax
from jax.experimental import pallas as pl
from jax.experimental.pallas import tpu as pltpu
from jax.sharding import PartitionSpec as P

H = 8
DH = 128
D = H * DH
BLK = 64
WIN = 2
MEM = 4
PAIR = 2 * BLK
HALO = WIN * BLK
SPAN = PAIR + 2 * HALO
NEG_FILL = -1e30
SCALE = 1.0 / math.sqrt(DH)
EXP2_SCALE = SCALE * math.log2(math.e)

MESH = pl.DeviceIdType.MESH

NT = (((1,), (1,)), ((), ()))
NN = (((1,), (0,)), ((), ()))
TN = (((0,), (0,)), ((), ()))


def dot(a, b, dims):
    return lax.dot_general(a, b, dims, preferred_element_type=jnp.float32)


def across(a, b):
    return dot(a, b, TN)


def flipped(number, mask):
    for bit in (1, 2, 4, 8, 16):
        if mask & bit:
            number = number + bit - 2 * bit * (number // bit % 2)
    return number


CORE, X, Y, Z, ZZ = 1, 2, 4, 8, 24
COLUMN = (0, Z, ZZ, Z ^ ZZ)


def gather_steps():
    steps = [(0, None, (Z, ZZ, X, Y, CORE))]
    steps += [(Z, None, (X, Y, CORE)), (ZZ, None, (Z, X, Y, CORE))]
    steps += [(X, None, ()), (Y, None, ()), (Z ^ ZZ, None, (X, Y, CORE))]
    steps += [(side ^ k, None, ()) for k in COLUMN[1:] for side in (X, Y)]
    steps += [(X ^ Y ^ k, half, (CORE,)) for k in COLUMN for half in (0, 1)]
    return steps


def sends():
    groups = []
    for block, half, partners in gather_steps():
        group = [(block, half, partner) for partner in partners]
        if block in [X ^ k for k in COLUMN]:
            group = [(block, 0, Y), (block, None, CORE)]
        if block in [Y ^ k for k in COLUMN]:
            group = [(block, 1, X), (block, None, CORE)]
        groups.append((block, half, group))
    return groups


def exchange_kernel(mem_ref, own_ref, table_ref, left_ref, right_ref, local_sem, send_sems, recv_sems, halo_sems, *, size, gather):
    me = lax.axis_index("seq")
    after, before = lax.rem(me + 1, size), lax.rem(me + size - 1, size)
    masks = (CORE, X, Y, Z, ZZ) if gather else ()
    barrier = pltpu.get_barrier_semaphore()
    partners = [flipped(me, mask) for mask in masks] + [after, before]
    for partner in partners:
        pl.semaphore_signal(barrier, inc=1, device_id=(partner,), device_id_type=MESH)
    pl.semaphore_wait(barrier, len(partners))

    rows = own_ref.shape[0]
    halos = [
        pltpu.make_async_remote_copy(
            src_ref=own_ref.at[pl.ds(start, HALO)], dst_ref=dst,
            send_sem=halo_sems.at[2 * i], recv_sem=halo_sems.at[2 * i + 1],
            device_id=(target,), device_id_type=MESH,
        )
        for i, (start, dst, target) in enumerate(
            ((rows - HALO, left_ref, after), (0, right_ref, before))
        )
    ]
    if not gather:
        for halo in halos:
            halo.start()
        for halo in halos:
            halo.wait()
        return
    blocks = mem_ref.shape[0]

    def part(half):
        return (0, blocks) if half is None else (half * (blocks // 2), blocks // 2)

    def slot(block, half):
        start, length = part(half)
        return table_ref.at[pl.ds(flipped(me, block) * blocks + start, length)]

    def copy(block, half, partner, number):
        start, length = part(half)
        target = slot(block, half)
        return pltpu.make_async_remote_copy(
            src_ref=mem_ref.at[pl.ds(start, length)] if block == 0 else target,
            dst_ref=target,
            send_sem=send_sems.at[number],
            recv_sem=recv_sems.at[2 * (block ^ partner) + (half or 0)],
            device_id=(flipped(me, partner),), device_id_type=MESH,
        )

    def arrived(block, half):
        target = slot(block, half)
        pltpu.make_async_remote_copy(
            src_ref=target, dst_ref=target, send_sem=send_sems.at[0],
            recv_sem=recv_sems.at[2 * block + (half or 0)],
            device_id=(flipped(me, CORE),), device_id_type=MESH,
        ).wait_recv()

    kept = pltpu.make_async_copy(mem_ref, slot(0, None), local_sem)
    kept.start()
    started = []
    for block, half, group in sends():
        if block:
            arrived(block, half)
        for b, h, partner in group:
            started.append(copy(b, h, partner, len(started)))
            started[-1].start()
        if block == 0:
            for halo in halos:
                halo.start()
    for block, half, group in sends():
        arrived(block ^ CORE, half)
    for one in started:
        one.wait_send()
    kept.wait()
    for halo in halos:
        halo.wait()


def exchange(memory, own, size, gather):
    count = sum(len(group) for _, _, group in sends())
    whole = memory.shape[0] * (size if gather else 1)
    anywhere = pl.BlockSpec(memory_space=pl.ANY)
    return pl.pallas_call(
        functools.partial(exchange_kernel, size=size, gather=gather),
        in_specs=[anywhere] * 2,
        out_specs=[anywhere] * 3,
        out_shape=[
            jax.ShapeDtypeStruct((whole,) + memory.shape[1:], memory.dtype),
            jax.ShapeDtypeStruct((HALO, 2 * D), own.dtype),
            jax.ShapeDtypeStruct((HALO, 2 * D), own.dtype),
        ],
        scratch_shapes=[
            pltpu.SemaphoreType.DMA,
            pltpu.SemaphoreType.DMA((count,)),
            pltpu.SemaphoreType.DMA((64,)),
            pltpu.SemaphoreType.DMA((4,)),
        ],
        compiler_params=pltpu.CompilerParams(collective_id=0, has_side_effects=True),
        name="exchange",
    )(memory, own)


def attention_kernel(
    regions_ref, slot_ref, me_ref, q_ref, do_ref, left_ref, own_ref, right_ref, far_ref,
    att_ref, dq_ref, dleft_ref, dkv_ref, dright_ref,
    kv, acc, table_ref, sems, *, pairs, size,
):
    step = pl.program_id(0)

    rows, stored = own_ref.shape[0], far_ref.shape[0] // 2
    near = SPAN - HALO
    first = [
        pltpu.make_async_copy(left_ref, kv.at[pl.ds(0, HALO)], sems.at[0]),
        pltpu.make_async_copy(own_ref.at[pl.ds(0, near)], kv.at[pl.ds(HALO, near)], sems.at[1]),
        pltpu.make_async_copy(far_ref.at[pl.ds(0, stored)], table_ref.at[pl.ds(0, stored)], sems.at[2]),
        pltpu.make_async_copy(
            far_ref.at[pl.ds(stored, stored)], table_ref.at[pl.ds(stored, stored)], sems.at[3]
        ),
    ]
    later = [
        pltpu.make_async_copy(
            own_ref.at[pl.ds(near, rows - near)],
            kv.at[pl.ds(HALO + near, rows - near)],
            sems.at[4],
        ),
        pltpu.make_async_copy(right_ref, kv.at[pl.ds(HALO + rows, HALO)], sems.at[5]),
    ]

    @pl.when(step == 0)
    def _():
        for copy in first + later:
            copy.start()
        acc[pl.ds(0, SPAN - PAIR), :] = jnp.zeros((SPAN - PAIR, 2 * D), jnp.float32)
        for copy in first:
            copy.wait()

    @pl.when(step == 1)
    def _():
        for copy in later:
            copy.wait()

    @pl.when(step < pairs)
    def _():
        base = pl.multiple_of(step * PAIR, PAIR)
        window = pl.ds(base, SPAN)
        row = lax.broadcasted_iota(jnp.int32, (PAIR, PAIR), 0)
        lane = lax.broadcasted_iota(jnp.int32, (PAIR, PAIR), 1)
        no_left = jnp.logical_and(step == 0, me_ref[0] == 0)
        no_right = jnp.logical_and(step == pairs - 1, me_ref[0] == size - 1)
        bias_left = jnp.where(
            jnp.logical_and(jnp.logical_or(row < BLK, lane >= BLK), jnp.logical_not(no_left)),
            0.0, NEG_FILL,
        )
        bias_right = jnp.where(
            jnp.logical_and(jnp.logical_or(row >= BLK, lane < BLK), jnp.logical_not(no_right)),
            0.0, NEG_FILL,
        )

        mem_keys, mem_values = [], []
        for b in range(2):
            parts = [table_ref[slot_ref[regions_ref[step * 2 + b, m]]] for m in range(MEM)]
            rows = jnp.concatenate(parts, axis=0)
            mem_keys.append(rows[:, :DH])
            mem_values.append(rows[:, DH:])

        def cols(h):
            return slice(h * DH, (h + 1) * DH)

        def stack(per_head):
            return [
                jnp.concatenate([x[b * BLK : (b + 1) * BLK] for x in per_head], axis=0)
                for b in range(2)
            ]

        def unstack(stacked, h):
            return jnp.concatenate([s[h * BLK : (h + 1) * BLK] for s in stacked], axis=0)

        q = [q_ref[:, cols(h)] for h in range(H)]
        mem_scores = [dot(x, k, NT) for x, k in zip(stack(q), mem_keys)]
        e_win, e_mem, p_win, p_mem, totals, out_win = [], [], [], [], [], []
        for h in range(H):
            sw = dot(q[h], kv[window, cols(h)], NT)
            sw = jnp.concatenate(
                [sw[:, :PAIR] + bias_left, sw[:, PAIR : 2 * PAIR], sw[:, 2 * PAIR :] + bias_right],
                axis=1,
            )
            sm = unstack(mem_scores, h)
            top = jnp.maximum(
                jnp.max(sw, axis=1, keepdims=True), jnp.max(sm, axis=1, keepdims=True)
            )
            ew = jnp.exp2((sw - top) * EXP2_SCALE)
            em = jnp.exp2((sm - top) * EXP2_SCALE)
            totals.append(jnp.sum(ew, axis=1, keepdims=True) + jnp.sum(em, axis=1, keepdims=True))
            e_win.append(ew)
            e_mem.append(em)
            p_win.append(ew.astype(jnp.bfloat16))
            p_mem.append(em.astype(jnp.bfloat16))
            out_win.append(dot(p_win[h], kv[window, slice(D + h * DH, D + (h + 1) * DH)], NN))
        out_mem = [dot(x, v, NN) for x, v in zip(stack(p_mem), mem_values)]
        scaled, deltas = [], []
        for h in range(H):
            inverse = 1.0 / totals[h]
            out = (out_win[h] + unstack(out_mem, h)) * inverse
            att_ref[:, cols(h)] = out.astype(jnp.bfloat16)
            low = (do_ref[:, cols(h)].astype(jnp.float32) * inverse).astype(jnp.bfloat16)
            scaled.append(low)
            deltas.append(jnp.sum(low.astype(jnp.float32) * out, axis=1, keepdims=True))
        mem_probs = [dot(x, v, NT) for x, v in zip(stack(scaled), mem_values)]
        ds_mem, dq_win = [], []
        for h in range(H):
            vcols = slice(D + h * DH, D + (h + 1) * DH)
            pw = dot(scaled[h], kv[window, vcols], NT)
            dsw = (e_win[h] * (pw - deltas[h])).astype(jnp.bfloat16)
            ds_mem.append((e_mem[h] * (unstack(mem_probs, h) - deltas[h])).astype(jnp.bfloat16))
            dq_win.append(dot(dsw, kv[window, cols(h)], NN))
            for columns, low, rows in ((cols(h), dsw, q[h]), (vcols, p_win[h], scaled[h])):
                term = across(low, rows)
                acc[pl.ds(base, SPAN - PAIR), columns] += term[: SPAN - PAIR]
                acc[pl.ds(base + SPAN - PAIR, PAIR), columns] = term[SPAN - PAIR :]
        dq_mem = [dot(x, k, NN) for x, k in zip(stack(ds_mem), mem_keys)]
        for h in range(H):
            dq_ref[:, cols(h)] = ((dq_win[h] + unstack(dq_mem, h)) * SCALE).astype(jnp.bfloat16)

    done = pl.ds(pl.multiple_of(step * PAIR, PAIR), PAIR)
    finished = jnp.concatenate(
        [(acc[done, :D] * SCALE).astype(jnp.bfloat16), acc[done, D:].astype(jnp.bfloat16)], axis=1
    )

    @pl.when(step == 0)
    def _():
        dleft_ref[...] = finished

    @pl.when(jnp.logical_and(step > 0, step <= pairs))
    def _():
        dkv_ref[...] = finished

    @pl.when(step == pairs + 1)
    def _():
        dright_ref[...] = finished


def attention(regions, slots, me, queries, grad_out, left, own, right, table, size):
    rows = queries.shape[0]
    pairs = rows // PAIR
    steps = pairs + 2 * HALO // PAIR
    ext = rows + 2 * HALO
    by_pair = pl.BlockSpec((PAIR, D), lambda i, *_: (jnp.minimum(i, pairs - 1), 0))
    spec = pltpu.PrefetchScalarGridSpec(
        num_scalar_prefetch=3,
        grid=(steps,),
        in_specs=[
            by_pair,
            by_pair,
            pl.BlockSpec(memory_space=pl.ANY),
            pl.BlockSpec(memory_space=pl.ANY),
            pl.BlockSpec(memory_space=pl.ANY),
            pl.BlockSpec(memory_space=pl.ANY),
        ],
        out_specs=[
            by_pair,
            by_pair,
            pl.BlockSpec((HALO, 2 * D), lambda i, *_: (0, 0)),
            pl.BlockSpec((PAIR, 2 * D), lambda i, *_: (jnp.clip(i - 1, 0, pairs - 1), 0)),
            pl.BlockSpec((HALO, 2 * D), lambda i, *_: (0, 0)),
        ],
        scratch_shapes=[
            pltpu.VMEM((ext, 2 * D), jnp.bfloat16),
            pltpu.VMEM((ext, 2 * D), jnp.float32),
            pltpu.VMEM(table.shape, table.dtype),
            pltpu.SemaphoreType.DMA((6,)),
        ],
    )
    return pl.pallas_call(
        functools.partial(attention_kernel, pairs=pairs, size=size),
        grid_spec=spec,
        out_shape=[
            jax.ShapeDtypeStruct((rows, D), jnp.bfloat16),
            jax.ShapeDtypeStruct((rows, D), jnp.bfloat16),
            jax.ShapeDtypeStruct((HALO, 2 * D), jnp.bfloat16),
            jax.ShapeDtypeStruct((rows, 2 * D), jnp.bfloat16),
            jax.ShapeDtypeStruct((HALO, 2 * D), jnp.bfloat16),
        ],
        compiler_params=pltpu.CompilerParams(vmem_limit_bytes=56 * 2**20),
        name="attention",
    )(regions, slots, me, queries, grad_out, left, own, right, table)


def per_device(queries, keys_values, memory, block_regions, region_slot, grad_out):
    rows = queries.shape[0]
    size = lax.axis_size("seq")
    me = lax.axis_index("seq")
    up = [(i, i + 1) for i in range(size - 1)]
    down = [(j, i) for i, j in up]
    own = keys_values.reshape(rows, 2 * D)
    gather = size == 32
    table, left, right = exchange(memory, own, size, gather)
    if not gather:
        table = lax.all_gather(memory, "seq", axis=0, tiled=True)
    attended, grad_queries, to_left, grads, to_right = attention(
        block_regions, region_slot, me.reshape(1), queries, grad_out, left, own, right, table, size
    )
    from_right = lax.ppermute(to_left, "seq", down)
    from_left = lax.ppermute(to_right, "seq", up)
    kept = lax.optimization_barrier(grads.reshape(rows, 2, D))
    for start, arrived in ((0, from_left), (rows - HALO, from_right)):
        total = kept[start : start + HALO].astype(jnp.float32) + arrived.reshape(
            HALO, 2, D
        ).astype(jnp.float32)
        kept = lax.dynamic_update_slice(kept, total.astype(jnp.bfloat16), (start, 0, 0))
    return attended, grad_queries, kept


def solution(mesh):
    placed = (
        P("seq", None),
        P("seq", None, None),
        P("seq", None, None),
        P("seq", None),
        P(),
        P("seq", None),
    )
    return jax.shard_map(
        per_device,
        mesh=mesh,
        in_specs=placed,
        out_specs=(P("seq", None), P("seq", None), P("seq", None, None)),
        check_vma=False,
    )
```
